32 devices in a mesh: grp: 2 (over core), fsdp: 8 (over z, x), tp: 2 (over y).
Axes of the slice: x: 2, y: 2, z: 4, core: 2. Of those that a mesh axis runs over, the one named last changes fastest.
Arguments:
- normed_inputs: bfloat16 [12288, 8192], P(('grp', 'fsdp')), may hold values from -6 to 6
- value_cotangent: bfloat16 [12288, 1024], P(('grp', 'fsdp'), 'tp'), may hold values from -0.0546875 to 0.0546875
- value_weight: bfloat16 [8192, 1024], P(('grp', 'fsdp'), 'tp'), may hold values from -0.0625 to 0.0625
- decode_inputs: bfloat16 [256, 4, 8192], P(('grp', 'fsdp'), None, 'tp'), may hold values from -6 to 6
- queries: bfloat16 [256, 4, 8192], P(('grp', 'fsdp'), None, 'tp')
- new_keys: bfloat16 [256, 4, 1024], P(('grp', 'fsdp'), None, 'tp'), may hold values from -6 to 6
- cache_keys: bfloat16 [256, 128, 1024], P(('grp', 'fsdp'), None, 'tp')
- cache_values: bfloat16 [256, 128, 1024], P(('grp', 'fsdp'), None, 'tp'), may hold values from -6 to 6
- lengths: int32 [256], P(('grp', 'fsdp')), may hold values from 2 to 128, as said below
Outputs:
- gradient: float32 [8192, 1024], P(('grp', 'fsdp'), 'tp')
- new_values: bfloat16 [256, 4, 1024], P(('grp', 'fsdp'), None, 'tp')
- attended: bfloat16 [256, 4, 8192], P(('grp', 'fsdp'), None, 'tp')
The draws below stay inside these ranges and needn't reach their ends.
Inputs may be any that keep to these rules, and one draw needn't show every extreme that they name: `lengths`: at least 2 and at most 128; some row has exactly 128.
All inputs are finite; a program needn't handle non-finite values.
Results may differ from the reference program's by a relative error of at most 0.0052.
Values may be sent and summed in bfloat16 or wider, within the bound.
A program may use at most 64 MiB of HBM per device.

```python
import math
import jax
import jax.numpy as jnp
from jax import lax

D = 8192
QH = 64
KVH = 8
HD = 128
CTX = 128
STEPS = 4
TOKENS = 12288
ROWS = 256


def draw_cache_keys(key, part):
    key = jax.random.fold_in(key, 3)
    drawn = jax.random.normal(key, (ROWS, CTX, KVH * HD), jnp.float32)
    return drawn.astype(jnp.bfloat16)


def draw_queries(key, part):
    key = jax.random.fold_in(key, 7)
    drawn = jax.random.normal(key, (ROWS, STEPS, QH * HD), jnp.float32)
    return drawn.astype(jnp.bfloat16)


def draw_lengths(key, part):
    key = jax.random.fold_in(key, 13)
    drawn = jax.random.randint(key, (ROWS,), 2, CTX + 1)
    return drawn.at[0].set(CTX).astype(jnp.int32)


def shard_levels(own_key, extent, cuts, least, high):
    def one(dim, parts):
        draws = jax.random.uniform(jax.random.fold_in(jax.random.fold_in(own_key, 6), dim), (parts,), jnp.float32, least / len(cuts), high / len(cuts))
        return jnp.repeat(jnp.exp(draws), extent[dim] // parts).reshape((-1,) + (1,) * (len(extent) - dim - 1))

    loudness = one(*cuts[0])
    for cut in cuts[1:]:
        loudness = loudness * one(*cut)
    return loudness


def scatter_about(rng, shape, spread, reach, pieces=(), held_as=jnp.bfloat16):
    factor_of = shard_levels(rng, shape, pieces, -0.22, 0.18) if pieces else 1.0
    array = jax.random.normal(rng, shape, jnp.float32) * spread * factor_of
    return jnp.minimum(jnp.maximum(array, -reach), reach).astype(held_as)


def setup_inputs(seed: int = 0) -> dict:
    key_of = jax.random.split(jax.random.key(seed), 10)
    return {
        "normed_inputs": scatter_about(key_of[0], (TOKENS, D), 1.0, 6.0, ((0, 16),)),
        "value_cotangent": scatter_about(key_of[1], (TOKENS, KVH * HD), TOKENS ** -0.5, 0.0546875, ((0, 16), (1, 2))),
        "value_weight": scatter_about(key_of[2], (D, KVH * HD), D ** -0.5, 0.0625, ((0, 16), (1, 2))),
        "decode_inputs": scatter_about(key_of[3], (ROWS, STEPS, D), 1.0, 6.0, ((0, 16), (2, 2))),
        "queries": draw_queries(jax.random.fold_in(key_of[9], 71), 0),
        "new_keys": scatter_about(key_of[5], (ROWS, STEPS, KVH * HD), 1.0, 6.0, ((0, 16), (2, 2))),
        "cache_keys": draw_cache_keys(jax.random.fold_in(key_of[9], 71), 0),
        "cache_values": scatter_about(key_of[7], (ROWS, CTX, KVH * HD), 1.0, 6.0, ((0, 16), (2, 2))),
        "lengths": draw_lengths(jax.random.fold_in(key_of[9], 71), 0),
    }


def attend_rows(queries, new_keys, new_values, cache_keys, cache_values, lengths):
    row_count = queries.shape[0]
    step_count = queries.shape[1]
    slot_count = cache_keys.shape[1]
    group_count = cache_keys.shape[2] // HD
    per_group = QH // KVH
    factor = 1.0 / math.sqrt(HD)
    query_heads = queries.reshape(row_count, step_count, group_count, per_group, HD).astype(jnp.float32)
    cached_keys = cache_keys.reshape(row_count, slot_count, group_count, HD).astype(jnp.float32)
    cached_values = cache_values.reshape(row_count, slot_count, group_count, HD).astype(jnp.float32)
    fresh_keys = new_keys.reshape(row_count, step_count, group_count, HD).astype(jnp.float32)
    fresh_values = new_values.reshape(row_count, step_count, group_count, HD).astype(jnp.float32)
    cache_scores = jnp.einsum('rsgqd,rpgd->rsgqp', query_heads, cached_keys) * factor
    live_slots = jnp.arange(slot_count, dtype=jnp.int32)[None, :] < lengths[:, None]
    cache_scores = jnp.where(live_slots[:, None, None, None, :], cache_scores, -1e+30)
    fresh_scores = jnp.einsum('rsgqd,rugd->rsgqu', query_heads, fresh_keys) * factor
    causal = jnp.arange(step_count, dtype=jnp.int32)[None, :] <= jnp.arange(step_count, dtype=jnp.int32)[:, None]
    fresh_scores = jnp.where(causal[None, :, None, None, :], fresh_scores, -1e+30)
    highest = jnp.maximum(lax.optimization_barrier(jnp.max(cache_scores, axis=-1)), lax.optimization_barrier(jnp.max(fresh_scores, axis=-1)))
    cache_exp = jnp.exp(cache_scores - highest[..., None])
    fresh_exp = jnp.exp(fresh_scores - highest[..., None])
    denominator = lax.optimization_barrier(jnp.sum(cache_exp, axis=-1)) + lax.optimization_barrier(jnp.sum(fresh_exp, axis=-1))
    cache_weights = (cache_exp / denominator[..., None]).astype(jnp.bfloat16)
    fresh_weights = (fresh_exp / denominator[..., None]).astype(jnp.bfloat16)
    mixed = jnp.einsum('rsgqp,rpgd->rsgqd', cache_weights.astype(jnp.float32), cached_values)
    mixed = mixed + jnp.einsum('rsgqu,rugd->rsgqd', fresh_weights.astype(jnp.float32), fresh_values)
    return mixed.astype(jnp.bfloat16).reshape(row_count, step_count, group_count * per_group * HD)

def reference(normed_inputs, value_cotangent, value_weight, decode_inputs, queries, new_keys, cache_keys, cache_values, lengths):
    gradient = lax.dot_general(normed_inputs, value_cotangent, (((0,), (0,)), ((), ())), preferred_element_type=jnp.float32)
    step_size = 0.4 / math.sqrt(D)
    updated = (value_weight.astype(jnp.float32) - step_size * gradient).astype(jnp.bfloat16)
    row_count = decode_inputs.shape[0]
    step_count = decode_inputs.shape[1]
    flat_inputs = decode_inputs.reshape(row_count * step_count, D)
    new_values = jnp.dot(flat_inputs, updated, preferred_element_type=jnp.float32).astype(jnp.bfloat16)
    new_values = new_values.reshape(row_count, step_count, updated.shape[1])
    attended = attend_rows(queries, new_keys, new_values, cache_keys, cache_values, lengths)
    return (gradient, new_values, attended)
```

```python
import functools
import math

import jax
import jax.numpy as jnp
from jax import lax
from jax.experimental import pallas as pl
from jax.experimental.pallas import tpu as pltpu
from jax.sharding import PartitionSpec as P

D = 8192
QH = 64
KVH = 8
HD = 128
LANES = 256
CHUNK = 128
MESH = pl.DeviceIdType.MESH
BF16 = jnp.bfloat16
F32 = jnp.float32


def attend_rows(queries, new_keys, new_values, cache_keys, cache_values, lengths):
    row_count = queries.shape[0]
    step_count = queries.shape[1]
    slot_count = cache_keys.shape[1]
    group_count = cache_keys.shape[2] // HD
    per_group = QH // KVH
    factor = 1.0 / math.sqrt(HD)
    query_heads = queries.reshape(row_count, step_count, group_count, per_group, HD)
    cached_keys = cache_keys.reshape(row_count, slot_count, group_count, HD)
    cached_values = cache_values.reshape(row_count, slot_count, group_count, HD)
    fresh_keys = new_keys.reshape(row_count, step_count, group_count, HD)
    fresh_values = new_values.reshape(row_count, step_count, group_count, HD)
    cache_scores = (
        jnp.einsum("rsgqd,rpgd->rsgqp", query_heads, cached_keys, preferred_element_type=F32)
        * factor
    )
    live_slots = jnp.arange(slot_count, dtype=jnp.int32)[None, :] < lengths[:, None]
    cache_scores = jnp.where(live_slots[:, None, None, None, :], cache_scores, -1e30)
    fresh_scores = (
        jnp.einsum("rsgqd,rugd->rsgqu", query_heads, fresh_keys, preferred_element_type=F32)
        * factor
    )
    causal = (
        jnp.arange(step_count, dtype=jnp.int32)[None, :]
        <= jnp.arange(step_count, dtype=jnp.int32)[:, None]
    )
    fresh_scores = jnp.where(causal[None, :, None, None, :], fresh_scores, -1e30)
    highest = jnp.maximum(jnp.max(cache_scores, axis=-1), jnp.max(fresh_scores, axis=-1))
    cache_exp = jnp.exp(cache_scores - highest[..., None])
    fresh_exp = jnp.exp(fresh_scores - highest[..., None])
    denominator = jnp.sum(cache_exp, axis=-1) + jnp.sum(fresh_exp, axis=-1)
    cache_weights = (cache_exp / denominator[..., None]).astype(BF16)
    fresh_weights = (fresh_exp / denominator[..., None]).astype(BF16)
    mixed = jnp.einsum(
        "rsgqp,rpgd->rsgqd", cache_weights, cached_values, preferred_element_type=F32
    )
    mixed = mixed + jnp.einsum(
        "rsgqu,rugd->rsgqd", fresh_weights, fresh_values, preferred_element_type=F32
    )
    return mixed.astype(BF16).reshape(row_count, step_count, group_count * per_group * HD)


def kernel(
    F, T, stages, x_hbm, dyt, w, dec, grad, nv,
    xbuf, acc, a_send, a_recv, decpos, u, nva, *rest
):
    n = 2 * F
    k_s = rest[: stages - 1]
    k_r = rest[stages - 1 : 2 * stages - 2]
    n_s = rest[2 * stages - 2 : 3 * stages - 2]
    n_r = rest[3 * stages - 2 : 4 * stages - 2]
    (x_sem, a_ssem, a_rsem, k_ssem, k_rsem, n_ssem, n_rsem, d_ssem, d_rsem, f_ssem, f_rsem,
     own_sem) = rest[4 * stages - 2 :]
    cols = dyt.shape[0]
    block = w.shape[0]
    halves = block // LANES
    parts = cols // CHUNK
    tokens = dec.shape[0]
    quarter = n // 4
    step_size = 0.4 / math.sqrt(D)
    g = lax.axis_index("grp")
    f = lax.axis_index("fsdp")
    t = lax.axis_index("tp")

    def place(p):
        g2 = 1 - g if (p >> (stages - 1)) & 1 else g
        f2 = f
        for bit in range(stages - 1):
            if (p >> (stages - 2 - bit)) & 1:
                f2 = f2 + (1 - 2 * ((f // (1 << bit)) % 2)) * (1 << bit)
        return g2, f2

    def partner(stage):
        return place(n >> (stage + 1)) + (t,)

    def x_copy(h, p):
        g2, f2 = place(p)
        start = pl.multiple_of((g2 * F + f2) * block + h * LANES, LANES)
        slot = h * n + p
        return pltpu.make_async_copy(
            x_hbm.at[:, pl.ds(start, LANES)], xbuf.at[slot], x_sem.at[slot]
        )

    order = [(h, q) for h in range(halves) for q in (3, 1)]
    order += [(h, q) for h in range(halves) for q in (2, 0)]
    for h, q in order:
        for p in range(q * quarter, (q + 1) * quarter):
            x_copy(h, p).start()

    barrier = pltpu.get_barrier_semaphore()
    for p in range(1, n):
        g2, f2 = place(p)
        pl.semaphore_signal(barrier, inc=1, device_id=(g2, f2, t), device_id_type=MESH)
    for d in range(1, T):
        pl.semaphore_signal(
            barrier, inc=1, device_id=(g, f, lax.rem(t + d, T)), device_id_type=MESH
        )
    pl.semaphore_wait(barrier, n - 1 + T - 1)

    share = n // T
    me = g * F + f
    is_root = me // share == t

    def dec_copy(p):
        g2, f2 = place(p)
        owner = g2 * F + f2
        start = pl.multiple_of((owner % share) * block, block)
        return owner // share == t, pltpu.make_async_remote_copy(
            src_ref=dec.at[:, pl.ds(start, block)],
            dst_ref=decpos.at[p],
            send_sem=d_ssem.at[p],
            recv_sem=d_rsem.at[p],
            device_id=(g2, f2, t),
            device_id_type=MESH,
        )

    own_start = pl.multiple_of((me % share) * block, block)
    own_copy = pltpu.make_async_copy(dec.at[:, pl.ds(own_start, block)], decpos.at[0], own_sem)

    @pl.when(is_root)
    def _():
        own_copy.start()

    for p in range(1, n):
        wanted, copy = dec_copy(p)
        pl.when(wanted)(copy.start)

    def forward(d):
        return pltpu.make_async_remote_copy(
            src_ref=decpos,
            dst_ref=decpos,
            send_sem=f_ssem.at[d],
            recv_sem=f_rsem,
            device_id=(g, f, lax.rem(t + d, T)),
            device_id_type=MESH,
        )

    def pass_on():
        @pl.when(is_root)
        def _():
            own_copy.wait()
            for p in range(1, n):
                dec_copy(p)[1].wait_recv()
            for d in range(1, T):
                forward(d).start()

    def multiply(h, q, store):
        for p in range(q * quarter, (q + 1) * quarter):
            x_copy(h, p).wait()

        def body(i, _):
            store(
                i,
                jnp.dot(dyt[...], xbuf[h * n + q * quarter + i], preferred_element_type=F32),
            )
            return 0

        lax.fori_loop(0, quarter, body, 0)

    def a_copy(h, q):
        return pltpu.make_async_remote_copy(
            src_ref=a_send.at[h, q],
            dst_ref=a_recv.at[h, q],
            send_sem=a_ssem.at[h, q],
            recv_sem=a_rsem.at[h, q],
            device_id=partner(0),
            device_id_type=MESH,
        )

    def for_partner(h, q):
        def store(i, value):
            a_send[h, q, i] = value.astype(BF16)

        multiply(h, q + 2, store)
        a_copy(h, q).start()

    def for_self(h, q):
        def store(i, value):
            acc[h, q * quarter + i] = value

        multiply(h, q, store)

    def k_copy(stage, c, h):
        k = c * halves + h
        return pltpu.make_async_remote_copy(
            src_ref=k_s[stage - 1].at[k],
            dst_ref=k_r[stage - 1].at[k],
            send_sem=k_ssem.at[stage - 1, k],
            recv_sem=k_rsem.at[stage - 1, k],
            device_id=partner(stage),
            device_id_type=MESH,
        )

    def first_send(c, h):
        cs = pl.ds(c * CHUNK, CHUNK)
        for i in range(quarter):
            k_s[0][c * halves + h, i] = (
                acc[h, quarter + i, cs, :] + a_recv[h, 1, i, cs, :].astype(F32)
            ).astype(BF16)
        k_copy(1, c, h).start()

    def reduce(stage, c, h):
        cs = pl.ds(c * CHUNK, CHUNK)
        k = c * halves + h
        count = n >> (stage + 1)
        k_copy(stage, c, h).wait_recv()
        if stage == 1 and c == 0:
            a_copy(h, 0).wait_recv()
        last = stage == stages - 1
        for i in range(count - 1, -1, -1):
            value = acc[h, i, cs, :] + k_r[stage - 1][k, i].astype(F32)
            if stage == 1:
                value = value + a_recv[h, 0, i, cs, :].astype(F32)
            if last:
                value = value.T
                hs = pl.ds(h * LANES, LANES)
                grad[hs, cs] = value
                u[hs, cs] = (w[hs, cs].astype(F32) - step_size * value).astype(BF16)
            elif i >= count // 2:
                k_s[stage][k, i - count // 2] = value.astype(BF16)
            else:
                acc[h, i, cs, :] = value
            if not last and i == count // 2:
                k_copy(stage + 1, c, h).start()

    def n_copy(stage, c):
        return pltpu.make_async_remote_copy(
            src_ref=n_s[stage].at[c],
            dst_ref=n_r[stage].at[c],
            send_sem=n_ssem.at[stage, c],
            recv_sem=n_rsem.at[stage, c],
            device_id=partner(stage),
            device_id_type=MESH,
        )

    def project(c):
        if c == 0:

            @pl.when(jnp.logical_not(is_root))
            def _():
                forward(1).wait_recv()

        cs = pl.ds(c * CHUNK, CHUNK)
        weight = u[:, cs]
        half = n // 2
        high = decpos[half:].reshape(half * tokens, block)
        n_s[0][c] = (
            jnp.dot(high, weight, preferred_element_type=F32)
            .astype(BF16)
            .reshape(half, tokens, CHUNK)
        )
        n_copy(0, c).start()
        low = decpos[:half].reshape(half * tokens, block)
        nva[c] = jnp.dot(low, weight, preferred_element_type=F32).reshape(half, tokens, CHUNK)

    def n_reduce(stage, c):
        count = n >> (stage + 1)
        n_copy(stage, c).wait_recv()
        value = nva[c, :count] + n_r[stage][c].astype(F32)
        if stage == stages - 1:
            nv[:, c * CHUNK : (c + 1) * CHUNK] = value[0].astype(BF16)
        else:
            n_s[stage + 1][c] = value[count // 2 :].astype(BF16)
            n_copy(stage + 1, c).start()
            nva[c, : count // 2] = value[: count // 2]

    chunks = [(c, h) for c in range(parts) for h in range(halves)]

    for_partner(0, 1)
    for_self(0, 1)
    for h in range(1, halves):
        for_partner(h, 1)
    a_copy(0, 1).wait_recv()
    first_send(0, 0)
    for h in range(1, halves):
        for_self(h, 1)
        a_copy(h, 1).wait_recv()
    for c, h in chunks[1:]:
        first_send(c, h)
    for h in range(halves):
        for_partner(h, 0)
    for h in range(halves):
        for_self(h, 0)
    pass_on()

    pending = []

    def slot():
        if pending:
            what, stage, c = pending.pop(0)
            if what == 0:
                project(c)
            else:
                n_reduce(stage, c)

    def finish(j):
        c, h = chunks[j]
        if h == halves - 1:
            pending.append((0, 0, c))
            pending.extend((1, s, c) for s in range(stages))

    def stage_of(stage, j):
        if 0 <= j < len(chunks):
            reduce(stage, *chunks[j])
            if stage == stages - 1:
                finish(j)

    for j in range(len(chunks) + stages):
        stage_of(1, j)
        for stage in range(3, stages):
            stage_of(stage, j - (stage - 2))
        slot()
        if j < len(chunks) - 1:
            slot()
        stage_of(2, j)
        slot()
    while pending:
        slot()

    for h in range(halves):
        for q in (0, 1):
            a_copy(h, q).wait_send()
    for c, h in chunks:
        for stage in range(1, stages):
            k_copy(stage, c, h).wait_send()
    for c in range(parts):
        for stage in range(stages):
            n_copy(stage, c).wait_send()
    for p in range(1, n):
        wanted, copy = dec_copy(p)
        pl.when(wanted)(copy.wait_send)

    @pl.when(is_root)
    def _():
        for d in range(1, T):
            forward(d).wait_send()


def exchange(F, T, x, dyt, w, dec):
    n = 2 * F
    stages = n.bit_length() - 1
    cols = dyt.shape[0]
    held = x.shape[0]
    block = w.shape[0]
    halves = block // LANES
    parts = cols // CHUNK
    tokens = dec.shape[0]
    count = halves * parts
    dma = pltpu.SemaphoreType.DMA
    k_bufs = [
        pltpu.VMEM((count, n >> (s + 1), CHUNK, LANES), BF16) for s in range(1, stages)
    ]
    n_bufs = [pltpu.VMEM((parts, n >> (s + 1), tokens, CHUNK), BF16) for s in range(stages)]
    vmem = pl.BlockSpec(memory_space=pltpu.VMEM)
    hbm = pl.BlockSpec(memory_space=pl.ANY)
    return pl.pallas_call(
        functools.partial(kernel, F, T, stages),
        out_shape=(
            jax.ShapeDtypeStruct((block, cols), F32),
            jax.ShapeDtypeStruct((tokens, cols), BF16),
        ),
        in_specs=[hbm, vmem, vmem, hbm],
        out_specs=(vmem, vmem),
        scratch_shapes=[
            pltpu.VMEM((halves * n, held, LANES), BF16),
            pltpu.VMEM((halves, n // 2, cols, LANES), F32),
            pltpu.VMEM((halves, 2, n // 4, cols, LANES), BF16),
            pltpu.VMEM((halves, 2, n // 4, cols, LANES), BF16),
            pltpu.VMEM((n, tokens, block), BF16),
            pltpu.VMEM((block, cols), BF16),
            pltpu.VMEM((parts, n // 2, tokens, CHUNK), F32),
            *k_bufs,
            *k_bufs,
            *n_bufs,
            *n_bufs,
            dma((halves * n,)),
            dma((halves, 2)),
            dma((halves, 2)),
            dma((stages - 1, count)),
            dma((stages - 1, count)),
            dma((stages, parts)),
            dma((stages, parts)),
            dma((n,)),
            dma((n,)),
            dma((T,)),
            dma,
            dma,
        ],
        compiler_params=pltpu.CompilerParams(
            collective_id=0, has_side_effects=True, vmem_limit_bytes=58 * 2**20
        ),
        cost_estimate=pl.CostEstimate(
            flops=2 * held * D * cols, bytes_accessed=held * D * 2, transcendentals=0
        ),
    )(x, dyt, w, dec)


def shards(
    F,
    T,
    normed_inputs,
    value_cotangent,
    value_weight,
    decode_inputs,
    queries,
    new_keys,
    cache_keys,
    cache_values,
    lengths,
):
    rows, steps, features = decode_inputs.shape
    gradient, flat_values = exchange(
        F,
        T,
        normed_inputs,
        value_cotangent.T,
        value_weight,
        decode_inputs.reshape(rows * steps, features),
    )
    new_values = flat_values.reshape(rows, steps, flat_values.shape[1])
    attended = attend_rows(queries, new_keys, new_values, cache_keys, cache_values, lengths)
    return (gradient, new_values, attended)


def solution(mesh):
    return jax.shard_map(
        functools.partial(shards, mesh.shape["fsdp"], mesh.shape["tp"]),
        mesh=mesh,
        in_specs=(
            P(("grp", "fsdp"), None),
            P(("grp", "fsdp"), "tp"),
            P(("grp", "fsdp"), "tp"),
            P(("grp", "fsdp"), None, "tp"),
            P(("grp", "fsdp"), None, "tp"),
            P(("grp", "fsdp"), None, "tp"),
            P(("grp", "fsdp"), None, "tp"),
            P(("grp", "fsdp"), None, "tp"),
            P(("grp", "fsdp")),
        ),
        out_specs=(
            P(("grp", "fsdp"), "tp"),
            P(("grp", "fsdp"), None, "tp"),
            P(("grp", "fsdp"), None, "tp"),
        ),
        check_vma=False,
    )
```

```python
import functools
import math

import jax
import jax.numpy as jnp
from jax import lax
from jax.experimental import pallas as pl
from jax.experimental.pallas import tpu as pltpu
from jax.sharding import PartitionSpec as P

D = 8192
QH = 64
KVH = 8
HD = 128
LANES = 256
CHUNK = 128
MESH = pl.DeviceIdType.MESH
BF16 = jnp.bfloat16
F32 = jnp.float32


def attend_rows(queries, new_keys, new_values, cache_keys, cache_values, lengths):
    row_count = queries.shape[0]
    step_count = queries.shape[1]
    slot_count = cache_keys.shape[1]
    group_count = cache_keys.shape[2] // HD
    per_group = QH // KVH
    factor = 1.0 / math.sqrt(HD)
    query_heads = queries.reshape(row_count, step_count, group_count, per_group, HD)
    cached_keys = cache_keys.reshape(row_count, slot_count, group_count, HD)
    cached_values = cache_values.reshape(row_count, slot_count, group_count, HD)
    fresh_keys = new_keys.reshape(row_count, step_count, group_count, HD)
    fresh_values = new_values.reshape(row_count, step_count, group_count, HD)
    cache_scores = (
        jnp.einsum("rsgqd,rpgd->rsgqp", query_heads, cached_keys, preferred_element_type=F32)
        * factor
    )
    live_slots = jnp.arange(slot_count, dtype=jnp.int32)[None, :] < lengths[:, None]
    cache_scores = jnp.where(live_slots[:, None, None, None, :], cache_scores, -1e30)
    fresh_scores = (
        jnp.einsum("rsgqd,rugd->rsgqu", query_heads, fresh_keys, preferred_element_type=F32)
        * factor
    )
    causal = (
        jnp.arange(step_count, dtype=jnp.int32)[None, :]
        <= jnp.arange(step_count, dtype=jnp.int32)[:, None]
    )
    fresh_scores = jnp.where(causal[None, :, None, None, :], fresh_scores, -1e30)
    highest = jnp.maximum(jnp.max(cache_scores, axis=-1), jnp.max(fresh_scores, axis=-1))
    cache_exp = jnp.exp(cache_scores - highest[..., None])
    fresh_exp = jnp.exp(fresh_scores - highest[..., None])
    denominator = jnp.sum(cache_exp, axis=-1) + jnp.sum(fresh_exp, axis=-1)
    cache_weights = (cache_exp / denominator[..., None]).astype(BF16)
    fresh_weights = (fresh_exp / denominator[..., None]).astype(BF16)
    mixed = jnp.einsum(
        "rsgqp,rpgd->rsgqd", cache_weights, cached_values, preferred_element_type=F32
    )
    mixed = mixed + jnp.einsum(
        "rsgqu,rugd->rsgqd", fresh_weights, fresh_values, preferred_element_type=F32
    )
    return mixed.astype(BF16).reshape(row_count, step_count, group_count * per_group * HD)


def kernel(
    F, T, stages, x_hbm, dyt, w, dec, grad, nv,
    xbuf, acc, a_send, a_recv, decpos, u, nva, *rest
):
    n = 2 * F
    k_s = rest[: stages - 1]
    k_r = rest[stages - 1 : 2 * stages - 2]
    n_s = rest[2 * stages - 2 : 3 * stages - 2]
    n_r = rest[3 * stages - 2 : 4 * stages - 2]
    (x_sem, a_ssem, a_rsem, k_ssem, k_rsem, n_ssem, n_rsem, d_ssem, d_rsem, f_ssem, f_rsem,
     own_sem) = rest[4 * stages - 2 :]
    cols = dyt.shape[0]
    block = w.shape[0]
    halves = block // LANES
    parts = cols // CHUNK
    tokens = dec.shape[0]
    quarter = n // 4
    step_size = 0.4 / math.sqrt(D)
    g = lax.axis_index("grp")
    f = lax.axis_index("fsdp")
    t = lax.axis_index("tp")

    def place(p):
        g2 = 1 - g if (p >> (stages - 1)) & 1 else g
        f2 = f
        for bit in range(stages - 1):
            if (p >> (stages - 2 - bit)) & 1:
                f2 = f2 + (1 - 2 * ((f // (1 << bit)) % 2)) * (1 << bit)
        return g2, f2

    def partner(stage):
        return place(n >> (stage + 1)) + (t,)

    def x_copy(h, p):
        g2, f2 = place(p)
        start = pl.multiple_of((g2 * F + f2) * block + h * LANES, LANES)
        slot = h * n + p
        return pltpu.make_async_copy(
            x_hbm.at[:, pl.ds(start, LANES)], xbuf.at[slot], x_sem.at[slot]
        )

    for h, q in [(h, q) for h in range(halves) for q in (3, 2, 1, 0)]:
        for p in range(q * quarter, (q + 1) * quarter):
            x_copy(h, p).start()

    barrier = pltpu.get_barrier_semaphore()
    for p in range(1, n):
        g2, f2 = place(p)
        pl.semaphore_signal(barrier, inc=1, device_id=(g2, f2, t), device_id_type=MESH)
    for d in range(1, T):
        pl.semaphore_signal(
            barrier, inc=1, device_id=(g, f, lax.rem(t + d, T)), device_id_type=MESH
        )
    pl.semaphore_wait(barrier, n - 1 + T - 1)

    share = n // T
    me = g * F + f
    is_root = me // share == t

    def dec_copy(p):
        g2, f2 = place(p)
        owner = g2 * F + f2
        start = pl.multiple_of((owner % share) * block, block)
        return owner // share == t, pltpu.make_async_remote_copy(
            src_ref=dec.at[:, pl.ds(start, block)],
            dst_ref=decpos.at[p],
            send_sem=d_ssem.at[p],
            recv_sem=d_rsem.at[p],
            device_id=(g2, f2, t),
            device_id_type=MESH,
        )

    own_start = pl.multiple_of((me % share) * block, block)
    own_copy = pltpu.make_async_copy(dec.at[:, pl.ds(own_start, block)], decpos.at[0], own_sem)

    @pl.when(is_root)
    def _():
        own_copy.start()

    for p in range(1, n):
        wanted, copy = dec_copy(p)
        pl.when(wanted)(copy.start)

    def forward(d):
        return pltpu.make_async_remote_copy(
            src_ref=decpos,
            dst_ref=decpos,
            send_sem=f_ssem.at[d],
            recv_sem=f_rsem,
            device_id=(g, f, lax.rem(t + d, T)),
            device_id_type=MESH,
        )

    def pass_on():
        @pl.when(is_root)
        def _():
            own_copy.wait()
            for p in range(1, n):
                dec_copy(p)[1].wait_recv()
            for d in range(1, T):
                forward(d).start()

    chunks = [(c, h) for c in range(parts) for h in range(halves)]

    def multiply(h, q, store):
        for p in range(q * quarter, (q + 1) * quarter):
            x_copy(h, p).wait()

        def body(i, _):
            store(
                i,
                jnp.dot(dyt[...], xbuf[h * n + q * quarter + i], preferred_element_type=F32),
            )
            return 0

        lax.fori_loop(0, quarter, body, 0)

    def a_copy(h, q):
        return pltpu.make_async_remote_copy(
            src_ref=a_send.at[h, q],
            dst_ref=a_recv.at[h, q],
            send_sem=a_ssem.at[h, q],
            recv_sem=a_rsem.at[h, q],
            device_id=partner(0),
            device_id_type=MESH,
        )

    def for_partner(h, q):
        def store(i, value):
            a_send[h, q, i] = value.astype(BF16)

        multiply(h, q + 2, store)
        a_copy(h, q).start()

    def for_self(h, q):
        def store(i, value):
            acc[h, q * quarter + i] = value

        multiply(h, q, store)

    def k_copy(stage, c, h):
        k = c * halves + h
        return pltpu.make_async_remote_copy(
            src_ref=k_s[stage - 1].at[k],
            dst_ref=k_r[stage - 1].at[k],
            send_sem=k_ssem.at[stage - 1, k],
            recv_sem=k_rsem.at[stage - 1, k],
            device_id=partner(plan(c, h)[stage - 1][0]),
            device_id_type=MESH,
        )

    def plan(c, h):
        bits = list(range(1, stages))
        if c == 0 and h == 0 and len(chunks) > 1:
            bits = bits[1:] + bits[:1]
        kept = list(range(n // 2))
        steps = []
        for bit in bits:
            mask = n >> (bit + 1)
            steps.append((bit, [p for p in kept if p & mask], [p for p in kept if not p & mask]))
            kept = steps[-1][2]
        return steps

    arrived = set()

    def paired(p, c, h):
        q = p // quarter
        if (h, q) not in arrived:
            a_copy(h, q).wait_recv()
            arrived.add((h, q))
        cs = pl.ds(c * CHUNK, CHUNK)
        return acc[h, p, cs, :] + a_recv[h, q, p % quarter, cs, :].astype(F32)

    def first_send(c, h):
        for i, p in enumerate(plan(c, h)[0][1]):
            k_s[0][c * halves + h, i] = paired(p, c, h).astype(BF16)
        k_copy(1, c, h).start()

    def reduce(stage, c, h):
        cs = pl.ds(c * CHUNK, CHUNK)
        k = c * halves + h
        steps = plan(c, h)
        kept = steps[stage - 1][2]
        last = stage == stages - 1
        going = [] if last else steps[stage][1]
        k_copy(stage, c, h).wait_recv()
        for p in going + [p for p in kept if p not in going]:
            value = paired(p, c, h) if stage == 1 else acc[h, p, cs, :]
            value = value + k_r[stage - 1][k, kept.index(p)].astype(F32)
            if last:
                value = value.T
                hs = pl.ds(h * LANES, LANES)
                grad[hs, cs] = value
                u[hs, cs] = (w[hs, cs].astype(F32) - step_size * value).astype(BF16)
            elif p in going:
                k_s[stage][k, going.index(p)] = value.astype(BF16)
                if p == going[-1]:
                    k_copy(stage + 1, c, h).start()
            else:
                acc[h, p, cs, :] = value

    def n_copy(stage, c):
        return pltpu.make_async_remote_copy(
            src_ref=n_s[stage].at[c],
            dst_ref=n_r[stage].at[c],
            send_sem=n_ssem.at[stage, c],
            recv_sem=n_rsem.at[stage, c],
            device_id=partner(stage),
            device_id_type=MESH,
        )

    def project(c):
        if c == 0:

            @pl.when(jnp.logical_not(is_root))
            def _():
                forward(1).wait_recv()

        cs = pl.ds(c * CHUNK, CHUNK)
        weight = u[:, cs]
        half = n // 2
        high = decpos[half:].reshape(half * tokens, block)
        n_s[0][c] = (
            jnp.dot(high, weight, preferred_element_type=F32)
            .astype(BF16)
            .reshape(half, tokens, CHUNK)
        )
        n_copy(0, c).start()
        low = decpos[:half].reshape(half * tokens, block)
        nva[c] = jnp.dot(low, weight, preferred_element_type=F32).reshape(half, tokens, CHUNK)

    def n_reduce(stage, c):
        count = n >> (stage + 1)
        n_copy(stage, c).wait_recv()
        value = nva[c, :count] + n_r[stage][c].astype(F32)
        if stage == stages - 1:
            nv[:, c * CHUNK : (c + 1) * CHUNK] = value[0].astype(BF16)
        else:
            n_s[stage + 1][c] = value[count // 2 :].astype(BF16)
            n_copy(stage + 1, c).start()
            nva[c, : count // 2] = value[: count // 2]

    sent = set()

    def send_chunk(j):
        if j < len(chunks) and j not in sent:
            sent.add(j)
            first_send(*chunks[j])

    for h in range(halves):
        for_partner(h, 1)
        for_partner(h, 0)
        for_self(h, 1)
        if h == 0:
            send_chunk(halves)
        else:
            send_chunk(h)
        for_self(h, 0)
        if h == 0:
            send_chunk(0)
    send_chunk(1)
    pass_on()

    pending = []

    def slot():
        if pending:
            what, stage, c = pending.pop(0)
            if what == 0:
                project(c)
            else:
                n_reduce(stage, c)

    def finish(j):
        c, h = chunks[j]
        if h == halves - 1:
            pending.append((0, 0, c))
            pending.extend((1, s, c) for s in range(stages))

    def stage_of(stage, j):
        if 0 <= j < len(chunks):
            reduce(stage, *chunks[j])
            if stage == stages - 1:
                finish(j)

    for j in range(len(chunks) + stages):
        stage_of(1, j)
        send_chunk(j + 3)
        for stage in range(3, stages):
            stage_of(stage, j - (stage - 2))
        slot()
        if j < len(chunks) - 1:
            slot()
        stage_of(2, j)
        slot()
    while pending:
        slot()

    for h in range(halves):
        for q in (0, 1):
            a_copy(h, q).wait_send()
    for c, h in chunks:
        for stage in range(1, stages):
            k_copy(stage, c, h).wait_send()
    for c in range(parts):
        for stage in range(stages):
            n_copy(stage, c).wait_send()
    for p in range(1, n):
        wanted, copy = dec_copy(p)
        pl.when(wanted)(copy.wait_send)

    @pl.when(is_root)
    def _():
        for d in range(1, T):
            forward(d).wait_send()


def exchange(F, T, x, dyt, w, dec):
    n = 2 * F
    stages = n.bit_length() - 1
    cols = dyt.shape[0]
    held = x.shape[0]
    block = w.shape[0]
    halves = block // LANES
    parts = cols // CHUNK
    tokens = dec.shape[0]
    count = halves * parts
    dma = pltpu.SemaphoreType.DMA
    k_bufs = [
        pltpu.VMEM((count, n >> (s + 1), CHUNK, LANES), BF16) for s in range(1, stages)
    ]
    n_bufs = [pltpu.VMEM((parts, n >> (s + 1), tokens, CHUNK), BF16) for s in range(stages)]
    vmem = pl.BlockSpec(memory_space=pltpu.VMEM)
    hbm = pl.BlockSpec(memory_space=pl.ANY)
    return pl.pallas_call(
        functools.partial(kernel, F, T, stages),
        out_shape=(
            jax.ShapeDtypeStruct((block, cols), F32),
            jax.ShapeDtypeStruct((tokens, cols), BF16),
        ),
        in_specs=[hbm, vmem, vmem, hbm],
        out_specs=(vmem, vmem),
        scratch_shapes=[
            pltpu.VMEM((halves * n, held, LANES), BF16),
            pltpu.VMEM((halves, n // 2, cols, LANES), F32),
            pltpu.VMEM((halves, 2, n // 4, cols, LANES), BF16),
            pltpu.VMEM((halves, 2, n // 4, cols, LANES), BF16),
            pltpu.VMEM((n, tokens, block), BF16),
            pltpu.VMEM((block, cols), BF16),
            pltpu.VMEM((parts, n // 2, tokens, CHUNK), F32),
            *k_bufs,
            *k_bufs,
            *n_bufs,
            *n_bufs,
            dma((halves * n,)),
            dma((halves, 2)),
            dma((halves, 2)),
            dma((stages - 1, count)),
            dma((stages - 1, count)),
            dma((stages, parts)),
            dma((stages, parts)),
            dma((n,)),
            dma((n,)),
            dma((T,)),
            dma,
            dma,
        ],
        compiler_params=pltpu.CompilerParams(
            collective_id=0, has_side_effects=True, vmem_limit_bytes=58 * 2**20
        ),
        cost_estimate=pl.CostEstimate(
            flops=2 * held * D * cols, bytes_accessed=held * D * 2, transcendentals=0
        ),
    )(x, dyt, w, dec)


def shards(
    F,
    T,
    normed_inputs,
    value_cotangent,
    value_weight,
    decode_inputs,
    queries,
    new_keys,
    cache_keys,
    cache_values,
    lengths,
):
    rows, steps, features = decode_inputs.shape
    gradient, flat_values = exchange(
        F,
        T,
        normed_inputs,
        value_cotangent.T,
        value_weight,
        decode_inputs.reshape(rows * steps, features),
    )
    new_values = flat_values.reshape(rows, steps, flat_values.shape[1])
    attended = attend_rows(queries, new_keys, new_values, cache_keys, cache_values, lengths)
    return (gradient, new_values, attended)


def solution(mesh):
    return jax.shard_map(
        functools.partial(shards, mesh.shape["fsdp"], mesh.shape["tp"]),
        mesh=mesh,
        in_specs=(
            P(("grp", "fsdp"), None),
            P(("grp", "fsdp"), "tp"),
            P(("grp", "fsdp"), "tp"),
            P(("grp", "fsdp"), None, "tp"),
            P(("grp", "fsdp"), None, "tp"),
            P(("grp", "fsdp"), None, "tp"),
            P(("grp", "fsdp"), None, "tp"),
            P(("grp", "fsdp"), None, "tp"),
            P(("grp", "fsdp")),
        ),
        out_specs=(
            P(("grp", "fsdp"), "tp"),
            P(("grp", "fsdp"), None, "tp"),
            P(("grp", "fsdp"), None, "tp"),
        ),
        check_vma=False,
    )
```

```python
import functools
import math

import jax
import jax.numpy as jnp
from jax import lax
from jax.experimental import pallas as pl
from jax.experimental.pallas import tpu as pltpu
from jax.sharding import PartitionSpec as P

D = 8192
QH = 64
KVH = 8
HD = 128
LANES = 256
CHUNK = 128
MESH = pl.DeviceIdType.MESH
BF16 = jnp.bfloat16
F32 = jnp.float32


def kernel(
    F, T, stages, x_hbm, dyt, w, dec, q_ref, nk, ck_hbm, cv_hbm, lengths, grad, nv, out,
    ck, cv, cache_sem, mixed, fresh, xbuf, acc, a_send, a_recv, decpos, u, nva, *rest
):
    n = 2 * F
    k_s = rest[: stages - 1]
    k_r = rest[stages - 1 : 2 * stages - 2]
    n_s = rest[2 * stages - 2 : 3 * stages - 2]
    n_r = rest[3 * stages - 2 : 4 * stages - 2]
    (x_sem, a_ssem, a_rsem, k_ssem, k_rsem, n_ssem, n_rsem, d_ssem, d_rsem, f_ssem, f_rsem,
     own_sem) = rest[4 * stages - 2 :]
    cols = dyt.shape[0]
    block = w.shape[0]
    halves = block // LANES
    parts = cols // CHUNK
    tokens = dec.shape[0]
    quarter = n // 4
    step_size = 0.4 / math.sqrt(D)
    g = lax.axis_index("grp")
    f = lax.axis_index("fsdp")
    t = lax.axis_index("tp")

    def place(p):
        g2 = 1 - g if (p >> (stages - 1)) & 1 else g
        f2 = f
        for bit in range(stages - 1):
            if (p >> (stages - 2 - bit)) & 1:
                f2 = f2 + (1 - 2 * ((f // (1 << bit)) % 2)) * (1 << bit)
        return g2, f2

    def partner(stage):
        return place(n >> (stage + 1)) + (t,)

    def x_copy(h, p):
        g2, f2 = place(p)
        start = pl.multiple_of((g2 * F + f2) * block + h * LANES, LANES)
        slot = h * n + p
        return pltpu.make_async_copy(
            x_hbm.at[:, pl.ds(start, LANES)], xbuf.at[slot], x_sem.at[slot]
        )

    for h, q in [(h, q) for h in range(halves) for q in (3, 2, 1, 0)]:
        for p in range(q * quarter, (q + 1) * quarter):
            x_copy(h, p).start()

    cache_copies = [
        pltpu.make_async_copy(ck_hbm, ck, cache_sem.at[0]),
        pltpu.make_async_copy(cv_hbm, cv, cache_sem.at[1]),
    ]
    for copy in cache_copies:
        copy.start()

    barrier = pltpu.get_barrier_semaphore()
    for p in range(1, n):
        g2, f2 = place(p)
        pl.semaphore_signal(barrier, inc=1, device_id=(g2, f2, t), device_id_type=MESH)
    for d in range(1, T):
        pl.semaphore_signal(
            barrier, inc=1, device_id=(g, f, lax.rem(t + d, T)), device_id_type=MESH
        )
    pl.semaphore_wait(barrier, n - 1 + T - 1)

    share = n // T
    me = g * F + f
    is_root = me // share == t

    def dec_copy(p):
        g2, f2 = place(p)
        owner = g2 * F + f2
        start = pl.multiple_of((owner % share) * block, block)
        return owner // share == t, pltpu.make_async_remote_copy(
            src_ref=dec.at[:, pl.ds(start, block)],
            dst_ref=decpos.at[p],
            send_sem=d_ssem.at[p],
            recv_sem=d_rsem.at[p],
            device_id=(g2, f2, t),
            device_id_type=MESH,
        )

    own_start = pl.multiple_of((me % share) * block, block)
    own_copy = pltpu.make_async_copy(dec.at[:, pl.ds(own_start, block)], decpos.at[0], own_sem)

    @pl.when(is_root)
    def _():
        own_copy.start()

    for p in range(1, n):
        wanted, copy = dec_copy(p)
        pl.when(wanted)(copy.start)

    def forward(d):
        return pltpu.make_async_remote_copy(
            src_ref=decpos,
            dst_ref=decpos,
            send_sem=f_ssem.at[d],
            recv_sem=f_rsem,
            device_id=(g, f, lax.rem(t + d, T)),
            device_id_type=MESH,
        )

    def pass_on():
        @pl.when(is_root)
        def _():
            own_copy.wait()
            for p in range(1, n):
                dec_copy(p)[1].wait_recv()
            for d in range(1, T):
                forward(d).start()

    chunks = [(c, h) for c in range(parts) for h in range(halves)]

    rows, groups, heads = q_ref.shape[:3]
    steps_per_row = tokens // rows
    factor = 1.0 / math.sqrt(HD)
    by_rows = (((1,), (1,)), ((), ()))

    def attend(r, _):
        slots = lax.broadcasted_iota(jnp.int32, (heads, ck.shape[1]), 1)
        live = slots < lengths[r]
        token = lax.broadcasted_iota(jnp.int32, (heads, tokens), 1) - r * steps_per_row
        step = lax.broadcasted_iota(jnp.int32, (heads, tokens), 0) >> 3
        causal = (token >= 0) & (token <= step)
        for group in range(groups):
            gs = pl.ds(group * HD, HD)
            query = q_ref[r, group]
            old = lax.dot_general(query, ck[r, :, gs], by_rows, preferred_element_type=F32)
            old = jnp.where(live, old * factor, -1e30)
            new = lax.dot_general(query, nk[:, gs], by_rows, preferred_element_type=F32)
            new = jnp.where(causal, new * factor, -1e30)
            highest = jnp.maximum(
                jnp.max(old, axis=-1, keepdims=True), jnp.max(new, axis=-1, keepdims=True)
            )
            old = jnp.exp(old - highest)
            new = jnp.exp(new - highest)
            total = jnp.sum(old, axis=-1, keepdims=True) + jnp.sum(new, axis=-1, keepdims=True)
            fresh[group, r] = (new / total).astype(BF16)
            mixed[group, r] = jnp.dot(
                (old / total).astype(BF16), cv[r, :, gs], preferred_element_type=F32
            )
        return 0

    def complete(group):
        weights = fresh[group].reshape(rows * heads, tokens)
        added = jnp.dot(
            weights, nv[:, group * HD : (group + 1) * HD], preferred_element_type=F32
        )
        out[group] = (mixed[group] + added.reshape(rows, heads, HD)).astype(BF16)

    def multiply(h, q, store):
        for p in range(q * quarter, (q + 1) * quarter):
            x_copy(h, p).wait()

        def body(i, _):
            store(
                i,
                jnp.dot(dyt[...], xbuf[h * n + q * quarter + i], preferred_element_type=F32),
            )
            return 0

        lax.fori_loop(0, quarter, body, 0)

    def a_copy(h, q):
        return pltpu.make_async_remote_copy(
            src_ref=a_send.at[h, q],
            dst_ref=a_recv.at[h, q],
            send_sem=a_ssem.at[h, q],
            recv_sem=a_rsem.at[h, q],
            device_id=partner(0),
            device_id_type=MESH,
        )

    def for_partner(h, q):
        def store(i, value):
            a_send[h, q, i] = value.astype(BF16)

        multiply(h, q + 2, store)
        a_copy(h, q).start()

    def for_self(h, q):
        def store(i, value):
            acc[h, q * quarter + i] = value

        multiply(h, q, store)

    def k_copy(stage, c, h):
        k = c * halves + h
        return pltpu.make_async_remote_copy(
            src_ref=k_s[stage - 1].at[k],
            dst_ref=k_r[stage - 1].at[k],
            send_sem=k_ssem.at[stage - 1, k],
            recv_sem=k_rsem.at[stage - 1, k],
            device_id=partner(plan(c, h)[stage - 1][0]),
            device_id_type=MESH,
        )

    def plan(c, h):
        bits = list(range(1, stages))
        if c == 0 and h == 0 and len(chunks) > 1:
            bits = bits[1:] + bits[:1]
        kept = list(range(n // 2))
        steps = []
        for bit in bits:
            mask = n >> (bit + 1)
            steps.append((bit, [p for p in kept if p & mask], [p for p in kept if not p & mask]))
            kept = steps[-1][2]
        return steps

    arrived = set()

    def paired(p, c, h):
        q = p // quarter
        if (h, q) not in arrived:
            a_copy(h, q).wait_recv()
            arrived.add((h, q))
        cs = pl.ds(c * CHUNK, CHUNK)
        return acc[h, p, cs, :] + a_recv[h, q, p % quarter, cs, :].astype(F32)

    def first_send(c, h):
        for i, p in enumerate(plan(c, h)[0][1]):
            k_s[0][c * halves + h, i] = paired(p, c, h).astype(BF16)
        k_copy(1, c, h).start()

    def reduce(stage, c, h):
        cs = pl.ds(c * CHUNK, CHUNK)
        k = c * halves + h
        steps = plan(c, h)
        kept = steps[stage - 1][2]
        last = stage == stages - 1
        going = [] if last else steps[stage][1]
        k_copy(stage, c, h).wait_recv()
        for p in going + [p for p in kept if p not in going]:
            value = paired(p, c, h) if stage == 1 else acc[h, p, cs, :]
            value = value + k_r[stage - 1][k, kept.index(p)].astype(F32)
            if last:
                value = value.T
                hs = pl.ds(h * LANES, LANES)
                grad[hs, cs] = value
                u[hs, cs] = (w[hs, cs].astype(F32) - step_size * value).astype(BF16)
            elif p in going:
                k_s[stage][k, going.index(p)] = value.astype(BF16)
                if p == going[-1]:
                    k_copy(stage + 1, c, h).start()
            else:
                acc[h, p, cs, :] = value

    def n_copy(stage, c):
        return pltpu.make_async_remote_copy(
            src_ref=n_s[stage].at[c],
            dst_ref=n_r[stage].at[c],
            send_sem=n_ssem.at[stage, c],
            recv_sem=n_rsem.at[stage, c],
            device_id=partner(stage),
            device_id_type=MESH,
        )

    def project(c):
        if c == 0:

            @pl.when(jnp.logical_not(is_root))
            def _():
                forward(1).wait_recv()

        cs = pl.ds(c * CHUNK, CHUNK)
        weight = u[:, cs]
        half = n // 2
        high = decpos[half:].reshape(half * tokens, block)
        n_s[0][c] = (
            jnp.dot(high, weight, preferred_element_type=F32)
            .astype(BF16)
            .reshape(half, tokens, CHUNK)
        )
        n_copy(0, c).start()
        low = decpos[:half].reshape(half * tokens, block)
        nva[c] = jnp.dot(low, weight, preferred_element_type=F32).reshape(half, tokens, CHUNK)

    def n_reduce(stage, c):
        count = n >> (stage + 1)
        n_copy(stage, c).wait_recv()
        value = nva[c, :count] + n_r[stage][c].astype(F32)
        if stage == stages - 1:
            nv[:, c * CHUNK : (c + 1) * CHUNK] = value[0].astype(BF16)
            ready.append(c)
            flush()
        else:
            n_s[stage + 1][c] = value[count // 2 :].astype(BF16)
            n_copy(stage + 1, c).start()
            nva[c, : count // 2] = value[: count // 2]

    sent = set()

    def send_chunk(j):
        if j < len(chunks) and j not in sent:
            sent.add(j)
            first_send(*chunks[j])

    for h in range(halves):
        for_partner(h, 1)
        for_partner(h, 0)
        for_self(h, 1)
        if h == 0:
            send_chunk(halves)
        else:
            send_chunk(h)
        for_self(h, 0)
        if h == 0:
            send_chunk(0)
    send_chunk(1)
    pass_on()

    ready = []
    attended_rows = [0]

    def flush():
        while ready and attended_rows[0] == rows:
            complete(ready.pop(0))

    def attend_some(count):
        first = attended_rows[0]
        if first < rows:
            attended_rows[0] = min(rows, first + count)
            lax.fori_loop(first, attended_rows[0], attend, 0)
        flush()

    pending = []

    def slot():
        if pending:
            what, stage, c = pending.pop(0)
            if what == 0:
                project(c)
            else:
                n_reduce(stage, c)

    def finish(j):
        c, h = chunks[j]
        if h == halves - 1:
            pending.append((0, 0, c))
            pending.extend((1, s, c) for s in range(stages))

    def stage_of(stage, j):
        if 0 <= j < len(chunks):
            reduce(stage, *chunks[j])
            if stage == stages - 1:
                finish(j)

    for copy in cache_copies:
        copy.wait()
    portion = -(-rows // max(1, parts * halves - 3))
    for j in range(len(chunks) + stages):
        stage_of(1, j)
        send_chunk(j + 3)
        for stage in range(3, stages):
            stage_of(stage, j - (stage - 2))
        slot()
        if j < len(chunks) - 1:
            slot()
        attend_some(portion)
        stage_of(2, j)
        slot()
    attend_some(rows)
    while pending:
        slot()

    for h in range(halves):
        for q in (0, 1):
            a_copy(h, q).wait_send()
    for c, h in chunks:
        for stage in range(1, stages):
            k_copy(stage, c, h).wait_send()
    for c in range(parts):
        for stage in range(stages):
            n_copy(stage, c).wait_send()
    for p in range(1, n):
        wanted, copy = dec_copy(p)
        pl.when(wanted)(copy.wait_send)

    @pl.when(is_root)
    def _():
        for d in range(1, T):
            forward(d).wait_send()


def exchange(F, T, x, dyt, w, dec, q, nk, ck, cv, lengths):
    n = 2 * F
    stages = n.bit_length() - 1
    cols = dyt.shape[0]
    held = x.shape[0]
    block = w.shape[0]
    halves = block // LANES
    parts = cols // CHUNK
    tokens = dec.shape[0]
    count = halves * parts
    rows, groups, heads = q.shape[:3]
    dma = pltpu.SemaphoreType.DMA
    k_bufs = [
        pltpu.VMEM((count, n >> (s + 1), CHUNK, LANES), BF16) for s in range(1, stages)
    ]
    n_bufs = [pltpu.VMEM((parts, n >> (s + 1), tokens, CHUNK), BF16) for s in range(stages)]
    vmem = pl.BlockSpec(memory_space=pltpu.VMEM)
    hbm = pl.BlockSpec(memory_space=pl.ANY)
    return pl.pallas_call(
        functools.partial(kernel, F, T, stages),
        out_shape=(
            jax.ShapeDtypeStruct((block, cols), F32),
            jax.ShapeDtypeStruct((tokens, cols), BF16),
            jax.ShapeDtypeStruct((groups, rows, heads, HD), BF16),
        ),
        in_specs=[
            hbm, vmem, vmem, hbm, vmem, vmem, hbm, hbm,
            pl.BlockSpec(memory_space=pltpu.SMEM),
        ],
        out_specs=(vmem, vmem, vmem),
        scratch_shapes=[
            pltpu.VMEM(ck.shape, BF16),
            pltpu.VMEM(cv.shape, BF16),
            dma((2,)),
            pltpu.VMEM((groups, rows, heads, HD), F32),
            pltpu.VMEM((groups, rows, heads, tokens), BF16),
            pltpu.VMEM((halves * n, held, LANES), BF16),
            pltpu.VMEM((halves, n // 2, cols, LANES), F32),
            pltpu.VMEM((halves, 2, n // 4, cols, LANES), BF16),
            pltpu.VMEM((halves, 2, n // 4, cols, LANES), BF16),
            pltpu.VMEM((n, tokens, block), BF16),
            pltpu.VMEM((block, cols), BF16),
            pltpu.VMEM((parts, n // 2, tokens, CHUNK), F32),
            *k_bufs,
            *k_bufs,
            *n_bufs,
            *n_bufs,
            dma((halves * n,)),
            dma((halves, 2)),
            dma((halves, 2)),
            dma((stages - 1, count)),
            dma((stages - 1, count)),
            dma((stages, parts)),
            dma((stages, parts)),
            dma((n,)),
            dma((n,)),
            dma((T,)),
            dma,
            dma,
        ],
        compiler_params=pltpu.CompilerParams(
            collective_id=0, has_side_effects=True, vmem_limit_bytes=58 * 2**20
        ),
        cost_estimate=pl.CostEstimate(
            flops=2 * held * D * cols, bytes_accessed=held * D * 2, transcendentals=0
        ),
    )(x, dyt, w, dec, q, nk, ck, cv, lengths)


def shards(
    F,
    T,
    normed_inputs,
    value_cotangent,
    value_weight,
    decode_inputs,
    queries,
    new_keys,
    cache_keys,
    cache_values,
    lengths,
):
    rows, steps, features = decode_inputs.shape
    groups = new_keys.shape[2] // HD
    per_group = QH // KVH
    by_group = queries.reshape(rows, steps, groups, per_group, HD).transpose(0, 2, 1, 3, 4)
    gradient, flat_values, mixed = exchange(
        F,
        T,
        normed_inputs,
        value_cotangent.T,
        value_weight,
        decode_inputs.reshape(rows * steps, features),
        by_group.reshape(rows, groups, steps * per_group, HD),
        new_keys.reshape(rows * steps, groups * HD),
        cache_keys,
        cache_values,
        lengths,
    )
    new_values = flat_values.reshape(rows, steps, flat_values.shape[1])
    attended = (
        mixed.reshape(groups, rows, steps, per_group, HD)
        .transpose(1, 2, 0, 3, 4)
        .reshape(rows, steps, groups * per_group * HD)
    )
    return (gradient, new_values, attended)


def solution(mesh):
    return jax.shard_map(
        functools.partial(shards, mesh.shape["fsdp"], mesh.shape["tp"]),
        mesh=mesh,
        in_specs=(
            P(("grp", "fsdp"), None),
            P(("grp", "fsdp"), "tp"),
            P(("grp", "fsdp"), "tp"),
            P(("grp", "fsdp"), None, "tp"),
            P(("grp", "fsdp"), None, "tp"),
            P(("grp", "fsdp"), None, "tp"),
            P(("grp", "fsdp"), None, "tp"),
            P(("grp", "fsdp"), None, "tp"),
            P(("grp", "fsdp")),
        ),
        out_specs=(
            P(("grp", "fsdp"), "tp"),
            P(("grp", "fsdp"), None, "tp"),
            P(("grp", "fsdp"), None, "tp"),
        ),
        check_vma=False,
    )
```

```python
import functools
import math

import jax
import jax.numpy as jnp
from jax import lax
from jax.experimental import pallas as pl
from jax.experimental.pallas import tpu as pltpu
from jax.sharding import PartitionSpec as P

D = 8192
QH = 64
KVH = 8
HD = 128
LANES = 256
CHUNK = 128
MESH = pl.DeviceIdType.MESH
BF16 = jnp.bfloat16
F32 = jnp.float32


def kernel(
    F, T, stages, x_hbm, dyt, w, dec, q_ref, nk, ck_hbm, cv_hbm, lengths, grad, nv, out,
    ck, cv, cache_sem, mixed, fresh, xbuf, acc, a_send, a_recv, decpos, u, nva, *rest
):
    n = 2 * F
    k_s = rest[: stages - 1]
    k_r = rest[stages - 1 : 2 * stages - 2]
    n_s = rest[2 * stages - 2 : 3 * stages - 2]
    n_r = rest[3 * stages - 2 : 4 * stages - 2]
    (x_sem, a_ssem, a_rsem, k_ssem, k_rsem, n_ssem, n_rsem, d_ssem, d_rsem, f_ssem, f_rsem,
     own_sem) = rest[4 * stages - 2 :]
    cols = dyt.shape[0]
    block = w.shape[0]
    halves = block // LANES
    parts = cols // CHUNK
    tokens = dec.shape[0]
    quarter = n // 4
    step_size = 0.4 / math.sqrt(D)
    g = lax.axis_index("grp")
    f = lax.axis_index("fsdp")
    t = lax.axis_index("tp")

    def place(p):
        g2 = 1 - g if (p >> (stages - 1)) & 1 else g
        f2 = f
        for bit in range(stages - 1):
            if (p >> (stages - 2 - bit)) & 1:
                f2 = f2 + (1 - 2 * ((f // (1 << bit)) % 2)) * (1 << bit)
        return g2, f2

    def partner(stage):
        return place(n >> (stage + 1)) + (t,)

    def x_copy(h, p):
        g2, f2 = place(p)
        start = pl.multiple_of((g2 * F + f2) * block + h * LANES, LANES)
        slot = h * n + p
        return pltpu.make_async_copy(
            x_hbm.at[:, pl.ds(start, LANES)], xbuf.at[slot], x_sem.at[slot]
        )

    for h, q in [(h, q) for h in range(halves) for q in (3, 2, 1, 0)]:
        for p in range(q * quarter, (q + 1) * quarter):
            x_copy(h, p).start()

    cache_copies = [
        pltpu.make_async_copy(ck_hbm, ck, cache_sem.at[0]),
        pltpu.make_async_copy(cv_hbm, cv, cache_sem.at[1]),
    ]
    for copy in cache_copies:
        copy.start()

    barrier = pltpu.get_barrier_semaphore()
    for p in range(1, n):
        g2, f2 = place(p)
        pl.semaphore_signal(barrier, inc=1, device_id=(g2, f2, t), device_id_type=MESH)
    for d in range(1, T):
        pl.semaphore_signal(
            barrier, inc=1, device_id=(g, f, lax.rem(t + d, T)), device_id_type=MESH
        )
    pl.semaphore_wait(barrier, n - 1 + T - 1)

    share = n // T
    me = g * F + f
    is_root = me // share == t

    def dec_copy(p):
        g2, f2 = place(p)
        owner = g2 * F + f2
        start = pl.multiple_of((owner % share) * block, block)
        return owner // share == t, pltpu.make_async_remote_copy(
            src_ref=dec.at[:, pl.ds(start, block)],
            dst_ref=decpos.at[p],
            send_sem=d_ssem.at[p],
            recv_sem=d_rsem.at[p],
            device_id=(g2, f2, t),
            device_id_type=MESH,
        )

    own_start = pl.multiple_of((me % share) * block, block)
    own_copy = pltpu.make_async_copy(dec.at[:, pl.ds(own_start, block)], decpos.at[0], own_sem)

    @pl.when(is_root)
    def _():
        own_copy.start()

    for p in range(1, n):
        wanted, copy = dec_copy(p)
        pl.when(wanted)(copy.start)

    def forward(d):
        return pltpu.make_async_remote_copy(
            src_ref=decpos,
            dst_ref=decpos,
            send_sem=f_ssem.at[d],
            recv_sem=f_rsem,
            device_id=(g, f, lax.rem(t + d, T)),
            device_id_type=MESH,
        )

    def pass_on():
        @pl.when(is_root)
        def _():
            own_copy.wait()
            for p in range(1, n):
                dec_copy(p)[1].wait_recv()
            for d in range(1, T):
                forward(d).start()

    chunks = [(c, h) for c in range(parts) for h in range(halves)]

    rows, groups, heads = q_ref.shape[:3]
    steps_per_row = tokens // rows
    factor = 1.0 / math.sqrt(HD)
    by_rows = (((1,), (1,)), ((), ()))

    def attend(r, _):
        slots = lax.broadcasted_iota(jnp.int32, (heads, ck.shape[1]), 1)
        live = slots < lengths[r]
        token = lax.broadcasted_iota(jnp.int32, (heads, tokens), 1) - r * steps_per_row
        step = lax.broadcasted_iota(jnp.int32, (heads, tokens), 0) >> 3
        causal = (token >= 0) & (token <= step)
        for group in range(groups):
            gs = pl.ds(group * HD, HD)
            query = q_ref[r, group]
            old = lax.dot_general(query, ck[r, :, gs], by_rows, preferred_element_type=F32)
            old = jnp.where(live, old * factor, -1e30)
            new = lax.dot_general(query, nk[:, gs], by_rows, preferred_element_type=F32)
            new = jnp.where(causal, new * factor, -1e30)
            highest = jnp.maximum(
                jnp.max(old, axis=-1, keepdims=True), jnp.max(new, axis=-1, keepdims=True)
            )
            old = jnp.exp(old - highest)
            new = jnp.exp(new - highest)
            total = jnp.sum(old, axis=-1, keepdims=True) + jnp.sum(new, axis=-1, keepdims=True)
            fresh[group, r] = (new / total).astype(BF16)
            mixed[group, r] = jnp.dot(
                (old / total).astype(BF16), cv[r, :, gs], preferred_element_type=F32
            )
        return 0

    def complete(group):
        weights = fresh[group].reshape(rows * heads, tokens)
        added = jnp.dot(
            weights, nv[:, group * HD : (group + 1) * HD], preferred_element_type=F32
        )
        out[group] = (mixed[group] + added.reshape(rows, heads, HD)).astype(BF16)

    def multiply(h, q, store):
        for p in range(q * quarter, (q + 1) * quarter):
            x_copy(h, p).wait()

        def body(i, _):
            store(
                i,
                jnp.dot(dyt[...], xbuf[h * n + q * quarter + i], preferred_element_type=F32),
            )
            return 0

        lax.fori_loop(0, quarter, body, 0)

    def a_copy(h, q):
        return pltpu.make_async_remote_copy(
            src_ref=a_send.at[h, q],
            dst_ref=a_recv.at[h, q],
            send_sem=a_ssem.at[h, q],
            recv_sem=a_rsem.at[h, q],
            device_id=partner(0),
            device_id_type=MESH,
        )

    def for_partner(h, q):
        def store(i, value):
            a_send[h, q, i] = value.astype(BF16)

        multiply(h, q + 2, store)
        a_copy(h, q).start()

    def for_self(h, q):
        def store(i, value):
            acc[h, q * quarter + i] = value

        multiply(h, q, store)

    def k_copy(stage, c, h):
        k = c * halves + h
        return pltpu.make_async_remote_copy(
            src_ref=k_s[stage - 1].at[k],
            dst_ref=k_r[stage - 1].at[k],
            send_sem=k_ssem.at[stage - 1, k],
            recv_sem=k_rsem.at[stage - 1, k],
            device_id=partner(plan(c, h)[stage - 1][0]),
            device_id_type=MESH,
        )

    def plan(c, h):
        bits = list(range(1, stages))
        if c == 0 and h == 0 and len(chunks) > 1:
            bits = bits[1:] + bits[:1]
        kept = list(range(n // 2))
        steps = []
        for bit in bits:
            mask = n >> (bit + 1)
            steps.append((bit, [p for p in kept if p & mask], [p for p in kept if not p & mask]))
            kept = steps[-1][2]
        return steps

    arrived = set()

    def paired(p, c, h):
        q = p // quarter
        if (h, q) not in arrived:
            a_copy(h, q).wait_recv()
            arrived.add((h, q))
        cs = pl.ds(c * CHUNK, CHUNK)
        return acc[h, p, cs, :] + a_recv[h, q, p % quarter, cs, :].astype(F32)

    def first_send(c, h):
        for i, p in enumerate(plan(c, h)[0][1]):
            k_s[0][c * halves + h, i] = paired(p, c, h).astype(BF16)
        k_copy(1, c, h).start()

    def reduce(stage, c, h):
        cs = pl.ds(c * CHUNK, CHUNK)
        k = c * halves + h
        steps = plan(c, h)
        kept = steps[stage - 1][2]
        last = stage == stages - 1
        going = [] if last else steps[stage][1]
        k_copy(stage, c, h).wait_recv()
        for p in going + [p for p in kept if p not in going]:
            value = paired(p, c, h) if stage == 1 else acc[h, p, cs, :]
            value = value + k_r[stage - 1][k, kept.index(p)].astype(F32)
            if last:
                value = value.T
                hs = pl.ds(h * LANES, LANES)
                grad[hs, cs] = value
                u[hs, cs] = (w[hs, cs].astype(F32) - step_size * value).astype(BF16)
            elif p in going:
                k_s[stage][k, going.index(p)] = value.astype(BF16)
                if p == going[-1]:
                    k_copy(stage + 1, c, h).start()
            else:
                acc[h, p, cs, :] = value

    def n_copy(stage, c):
        return pltpu.make_async_remote_copy(
            src_ref=n_s[stage].at[c],
            dst_ref=n_r[stage].at[c],
            send_sem=n_ssem.at[stage, c],
            recv_sem=n_rsem.at[stage, c],
            device_id=partner(stage),
            device_id_type=MESH,
        )

    def project(c):
        if c == 0:

            @pl.when(jnp.logical_not(is_root))
            def _():
                forward(1).wait_recv()

        cs = pl.ds(c * CHUNK, CHUNK)
        weight = u[:, cs]
        half = n // 2
        high = decpos[half:].reshape(half * tokens, block)
        n_s[0][c] = (
            jnp.dot(high, weight, preferred_element_type=F32)
            .astype(BF16)
            .reshape(half, tokens, CHUNK)
        )
        n_copy(0, c).start()
        low = decpos[:half].reshape(half * tokens, block)
        nva[c] = jnp.dot(low, weight, preferred_element_type=F32).reshape(half, tokens, CHUNK)

    def n_reduce(stage, c):
        count = n >> (stage + 1)
        n_copy(stage, c).wait_recv()
        value = nva[c, :count] + n_r[stage][c].astype(F32)
        if stage == stages - 1:
            nv[:, c * CHUNK : (c + 1) * CHUNK] = value[0].astype(BF16)
            ready.append(c)
            flush()
        else:
            n_s[stage + 1][c] = value[count // 2 :].astype(BF16)
            n_copy(stage + 1, c).start()
            nva[c, : count // 2] = value[: count // 2]

    sent = set()

    def send_chunk(j):
        if j < len(chunks) and j not in sent:
            sent.add(j)
            first_send(*chunks[j])

    for h in range(halves):
        for_partner(h, 1)
        for_partner(h, 0)
        for_self(h, 1)
        if h == 0:
            send_chunk(halves)
            send_chunk(2 * halves)
        else:
            send_chunk(h)
        for_self(h, 0)
        if h == 0:
            send_chunk(0)
    send_chunk(1)
    pass_on()

    ready = []
    attended_rows = [0]

    def flush():
        while ready and attended_rows[0] == rows:
            complete(ready.pop(0))

    def attend_some(count):
        first = attended_rows[0]
        if first < rows:
            attended_rows[0] = min(rows, first + count)
            lax.fori_loop(first, attended_rows[0], attend, 0)
        flush()

    pending = []

    def slot():
        if pending:
            what, stage, c = pending.pop(0)
            if what == 0:
                project(c)
            else:
                n_reduce(stage, c)

    def finish(j):
        c, h = chunks[j]
        if h == halves - 1:
            pending.append((0, 0, c))
            pending.extend((1, s, c) for s in range(stages))

    def stage_of(stage, j):
        if 0 <= j < len(chunks):
            reduce(stage, *chunks[j])
            if stage == stages - 1:
                finish(j)

    for copy in cache_copies:
        copy.wait()
    portion = -(-rows // max(1, parts * halves - 2))
    for j in range(len(chunks) + stages):
        stage_of(1, j)
        send_chunk(j + 3)
        if j < len(chunks):
            attend_some(portion)
        for stage in range(2, stages):
            stage_of(stage, j - (stage - 1))
            slot()
    attend_some(rows)
    while pending:
        slot()

    for h in range(halves):
        for q in (0, 1):
            a_copy(h, q).wait_send()
    for c, h in chunks:
        for stage in range(1, stages):
            k_copy(stage, c, h).wait_send()
    for c in range(parts):
        for stage in range(stages):
            n_copy(stage, c).wait_send()
    for p in range(1, n):
        wanted, copy = dec_copy(p)
        pl.when(wanted)(copy.wait_send)

    @pl.when(is_root)
    def _():
        for d in range(1, T):
            forward(d).wait_send()


def exchange(F, T, x, dyt, w, dec, q, nk, ck, cv, lengths):
    n = 2 * F
    stages = n.bit_length() - 1
    cols = dyt.shape[0]
    held = x.shape[0]
    block = w.shape[0]
    halves = block // LANES
    parts = cols // CHUNK
    tokens = dec.shape[0]
    count = halves * parts
    rows, groups, heads = q.shape[:3]
    dma = pltpu.SemaphoreType.DMA
    k_bufs = [
        pltpu.VMEM((count, n >> (s + 1), CHUNK, LANES), BF16) for s in range(1, stages)
    ]
    n_bufs = [pltpu.VMEM((parts, n >> (s + 1), tokens, CHUNK), BF16) for s in range(stages)]
    vmem = pl.BlockSpec(memory_space=pltpu.VMEM)
    hbm = pl.BlockSpec(memory_space=pl.ANY)
    return pl.pallas_call(
        functools.partial(kernel, F, T, stages),
        out_shape=(
            jax.ShapeDtypeStruct((block, cols), F32),
            jax.ShapeDtypeStruct((tokens, cols), BF16),
            jax.ShapeDtypeStruct((groups, rows, heads, HD), BF16),
        ),
        in_specs=[
            hbm, vmem, vmem, hbm, vmem, vmem, hbm, hbm,
            pl.BlockSpec(memory_space=pltpu.SMEM),
        ],
        out_specs=(vmem, vmem, vmem),
        scratch_shapes=[
            pltpu.VMEM(ck.shape, BF16),
            pltpu.VMEM(cv.shape, BF16),
            dma((2,)),
            pltpu.VMEM((groups, rows, heads, HD), F32),
            pltpu.VMEM((groups, rows, heads, tokens), BF16),
            pltpu.VMEM((halves * n, held, LANES), BF16),
            pltpu.VMEM((halves, n // 2, cols, LANES), F32),
            pltpu.VMEM((halves, 2, n // 4, cols, LANES), BF16),
            pltpu.VMEM((halves, 2, n // 4, cols, LANES), BF16),
            pltpu.VMEM((n, tokens, block), BF16),
            pltpu.VMEM((block, cols), BF16),
            pltpu.VMEM((parts, n // 2, tokens, CHUNK), F32),
            *k_bufs,
            *k_bufs,
            *n_bufs,
            *n_bufs,
            dma((halves * n,)),
            dma((halves, 2)),
            dma((halves, 2)),
            dma((stages - 1, count)),
            dma((stages - 1, count)),
            dma((stages, parts)),
            dma((stages, parts)),
            dma((n,)),
            dma((n,)),
            dma((T,)),
            dma,
            dma,
        ],
        compiler_params=pltpu.CompilerParams(
            collective_id=0, has_side_effects=True, vmem_limit_bytes=58 * 2**20
        ),
        cost_estimate=pl.CostEstimate(
            flops=2 * held * D * cols, bytes_accessed=held * D * 2, transcendentals=0
        ),
    )(x, dyt, w, dec, q, nk, ck, cv, lengths)


def shards(
    F,
    T,
    normed_inputs,
    value_cotangent,
    value_weight,
    decode_inputs,
    queries,
    new_keys,
    cache_keys,
    cache_values,
    lengths,
):
    rows, steps, features = decode_inputs.shape
    groups = new_keys.shape[2] // HD
    per_group = QH // KVH
    by_group = queries.reshape(rows, steps, groups, per_group, HD).transpose(0, 2, 1, 3, 4)
    gradient, flat_values, mixed = exchange(
        F,
        T,
        normed_inputs,
        value_cotangent.T,
        value_weight,
        decode_inputs.reshape(rows * steps, features),
        by_group.reshape(rows, groups, steps * per_group, HD),
        new_keys.reshape(rows * steps, groups * HD),
        cache_keys,
        cache_values,
        lengths,
    )
    new_values = flat_values.reshape(rows, steps, flat_values.shape[1])
    attended = (
        mixed.reshape(groups, rows, steps, per_group, HD)
        .transpose(1, 2, 0, 3, 4)
        .reshape(rows, steps, groups * per_group * HD)
    )
    return (gradient, new_values, attended)


def solution(mesh):
    return jax.shard_map(
        functools.partial(shards, mesh.shape["fsdp"], mesh.shape["tp"]),
        mesh=mesh,
        in_specs=(
            P(("grp", "fsdp"), None),
            P(("grp", "fsdp"), "tp"),
            P(("grp", "fsdp"), "tp"),
            P(("grp", "fsdp"), None, "tp"),
            P(("grp", "fsdp"), None, "tp"),
            P(("grp", "fsdp"), None, "tp"),
            P(("grp", "fsdp"), None, "tp"),
            P(("grp", "fsdp"), None, "tp"),
            P(("grp", "fsdp")),
        ),
        out_specs=(
            P(("grp", "fsdp"), "tp"),
            P(("grp", "fsdp"), None, "tp"),
            P(("grp", "fsdp"), None, "tp"),
        ),
        check_vma=False,
    )
```
